512 devices in a mesh: rep: 8 (over y_lo, core), shard: 64 (over y_hi, z, x).
Axes of the slice: x: 4, y: 8 (y_hi: 2, y_lo: 4; y = y_hi * 4 + y_lo), z: 8, core: 2. Of those that a mesh axis runs over, the one named last changes fastest.
Arguments:
- grad_parts: bfloat16 [8, 64, 576, 1152], P('rep', 'shard'), may hold values from -64 to 64
- master: float32 [576, 1152], P('shard'), may hold values from -0.06 to 0.06
- moment_one: float32 [576, 1152], P('shard'), may hold values from -0.12 to 0.12
- moment_two: float32 [576, 1152], P('shard'), may hold values from 0.0001 to 0.01
- step_count: int32 [1], replicated, may hold values from 1 to 20
Outputs:
- new_master: float32 [576, 1152], P('shard')
- new_moment_one: float32 [576, 1152], P('shard')
- new_moment_two: float32 [576, 1152], P('shard')
- adam_direction: float32 [576, 1152], P('shard')
- params: bfloat16 [576, 1152], replicated
The draws below stay inside these ranges and needn't reach their ends.
All inputs are finite; a program needn't handle non-finite values.
Results may differ from the reference program's by a relative error of at most 0.024.
Values may be sent and summed in bfloat16 or wider, within the bound.
A program may use at most 64 MiB of HBM per device.

```python
import math
import jax
import jax.numpy as jnp
from jax import lax

D = 1152
ROWS = 576
N_REP = 8
N_SHARD = 64


def spiked(values, key, source, target, blocks, factor):
    def block_of(axis_at):
        return (jnp.arange(values.shape[axis_at]) // (values.shape[axis_at] // blocks)).reshape((-1,) + (1,) * (values.ndim - 1 - axis_at))

    first = jax.random.permutation(key, blocks)[block_of(target)]
    second = (block_of(target) + blocks // 2) % blocks
    return jnp.where((block_of(source) == first) | (block_of(source) == second), factor * values, values)


def block_levels(key, dims, cuts, least, high):
    level, own = 1.0, jax.random.fold_in(key, 6)
    for position, parts in cuts:
        draws = jnp.exp(jax.random.uniform(jax.random.fold_in(own, position), (parts,), jnp.float32, least / len(cuts), high / len(cuts)))
        level = level * jnp.repeat(draws, dims[position] // parts).reshape([-1 if axis == position else 1 for axis in range(len(dims))])
    return level


def bell_draw(key, shape, deviation, reach, cuts=(), held_as=jnp.bfloat16):
    entries = deviation * jax.random.normal(key, shape, jnp.float32)
    if cuts:
        entries = entries * block_levels(key, shape, cuts, -0.22, 0.18)
    return jnp.clip(entries, -reach, reach).astype(held_as)


def noise_with(rng, dims, scale, most, shards, heavy, held_as=jnp.bfloat16):
    drawn = scale * jax.random.normal(rng, dims, jnp.float32)
    if shards:
        drawn = drawn * block_levels(rng, dims, shards, -0.22, 0.18)
    return jnp.clip(spiked(drawn, jax.random.fold_in(rng, 3), *heavy), -most, most).astype(held_as)


def setup_inputs(seed: int = 0) -> dict:
    seeds = jax.random.split(jax.random.key(seed), 6)
    return {
        "grad_parts": noise_with(seeds[0], (N_REP, N_SHARD, ROWS, D), 4.0, 64.0, ((0, 8), (1, 64)), (1, 2, 64, 4.0)),
        "master": bell_draw(seeds[1], (ROWS, D), 0.01, 0.06, ((0, 64),), jnp.float32),
        "moment_one": bell_draw(seeds[2], (ROWS, D), 0.02, 0.12, ((0, 64),), jnp.float32),
        "moment_two": jnp.clip(jnp.exp(math.log(0.01) - 4.6051702 * jax.random.uniform(seeds[3], (ROWS, D), jnp.float32) ** block_levels(seeds[3], (ROWS, D), ((0, 64),), -0.2, 0.2)), 0.0001, 0.01),
        "step_count": jax.random.randint(seeds[4], (1,), 1, 21).astype(jnp.int32),
    }


BETA_ONE = 0.9
BETA_TWO = 0.95
LEARN_RATE = 0.001
EPSILON = 1e-08

def reference(grad_parts, master, moment_one, moment_two, step_count):
    summed = lax.optimization_barrier(jnp.sum(grad_parts.astype(jnp.float32), axis=(0, 1)))
    gradient = summed / (N_REP * N_SHARD)
    new_moment_one = BETA_ONE * moment_one + (1.0 - BETA_ONE) * gradient
    new_moment_two = BETA_TWO * moment_two + (1.0 - BETA_TWO) * gradient * gradient
    steps_float = step_count[0].astype(jnp.float32)
    first_fix = 1.0 - jnp.power(jnp.float32(BETA_ONE), steps_float)
    second_fix = 1.0 - jnp.power(jnp.float32(BETA_TWO), steps_float)
    adam_direction = new_moment_one / first_fix / (jnp.sqrt(new_moment_two / second_fix) + EPSILON)
    new_master = master - LEARN_RATE * adam_direction
    params = new_master.astype(jnp.bfloat16)
    return (new_master, new_moment_one, new_moment_two, adam_direction, params)
```

```python
import math

import jax
import jax.numpy as jnp
from jax import lax
from jax.experimental import pallas as pl
from jax.experimental.pallas import tpu as pltpu
from jax.sharding import PartitionSpec as P

MESH = pl.DeviceIdType.MESH
F32, BF16 = jnp.float32, jnp.bfloat16
BETA_ONE = 0.9
BETA_TWO = 0.95
LEARN_RATE = 0.001
EPSILON = 1e-08

ROWS, D = 576, 1152
NA, NB = 6, 3
CA = NA * 128

LOC, S0, A1, B1, A2, B2, Y3, SIB, G1, GA2, GB2, GA3, GB3, FA, FB, END = (
    0, 4, 8, 12, 20, 28, 32, 40, 41, 42, 50, 54, 58, 66, 70, 74,
)


def kernel(
    grad, master, mom1, mom2, step,
    o_master, o_m1, o_m2, o_dir, o_par,
    own, sib, f, sa1, ra1, sb1, rb1, acc_a, acc_b, stage, sa2, ra2, sb2, rb2, s3, r3,
    gs, qs, pb2, gz, gx, ha, hb, o, send, recv,
):
    rep, shard = lax.axis_index("rep"), lax.axis_index("shard")
    c, y_lo = rep % 2, rep // 2
    x, z, y_hi = shard % 4, (shard // 4) % 8, shard // 32
    y = y_hi * 4 + y_lo
    z_lo = z % 4
    act = z // 4 == c

    def dev(x_, y_, z_, c_):
        return ((y_ % 4) * 2 + c_, (y_ // 4) * 32 + z_ * 4 + x_)

    def rdma(src, dst, ssem, rsem, where):
        return pltpu.make_async_remote_copy(
            src_ref=src, dst_ref=dst, send_sem=send.at[ssem], recv_sem=recv.at[rsem], device_id=where, device_id_type=MESH
        )

    sibling = dev(x, y, z, 1 - c)

    def wait_recv(ref, slot):
        rdma(ref, ref, slot, slot, sibling).wait_recv()

    def wait_send(ref, slot):
        rdma(ref, ref, slot, slot, sibling).wait_send()

    def own_copies(part):
        lo, n = ((CA, D - CA), (0, CA))[part]
        return [
            pltpu.make_async_copy(
                grad.at[pl.ds(pl.multiple_of(h * 288 + c * 144, 16), 144), pl.ds(lo, n)],
                own.at[h, :, pl.ds(lo, n)],
                recv.at[LOC + 2 * part + h],
            )
            for h in range(2)
        ]

    for part in range(2):
        for cp in own_copies(part):
            cp.start()

    barrier = pltpu.get_barrier_semaphore()

    def greet(where):
        pl.semaphore_signal(barrier, inc=1, device_id=where, device_id_type=MESH)

    greet(sibling)
    for d in range(1, 8):
        greet(dev(x, y, (z + d) % 8, c))
        greet(dev(x, (y + d) % 8, z, c))
    for d in range(1, 4):
        greet(dev((x + d) % 4, y, z, c))
    pl.semaphore_wait(barrier, 18)

    def sib_copies(part):
        lo, n = ((CA, D - CA), (0, CA))[part]
        return [
            rdma(
                grad.at[pl.ds(pl.multiple_of(h * 288 + (1 - c) * 144, 16), 144), pl.ds(lo, n)],
                sib.at[h, :, pl.ds(lo, n)],
                S0 + 2 * part + h, S0 + 2 * part + h, sibling,
            )
            for h in range(2)
        ]

    for part in range(2):
        for cp in sib_copies(part):
            cp.start()

    acc_a[pl.ds(432, 16), :] = jnp.zeros((16, 128), F32)
    acc_b[pl.ds(216, 40), :] = jnp.zeros((40, 128), F32)
    stage[pl.ds(216, 8), :] = jnp.zeros((8, 128), F32)

    def add_pair(part):
        for cp in own_copies(part):
            cp.wait()
        for cp in sib_copies(part):
            cp.wait_recv()
        for l in ((6, 7, 8), range(6))[part]:
            for h in range(2):
                cols = pl.ds(l * 128, 128)
                f[l, pl.ds(h * 144, 144), :] = own[h, :, cols].astype(F32) + sib[h, :, cols].astype(F32)

    add_pair(0)
    for j in range(4):
        for i in range(27):
            l, r = divmod(i, 9)
            for h in range(2):
                stage[pl.ds(i * 8 + h * 4, 4), :] = f[6 + l, pl.ds(h * 144 + j * 36 + r, 4, stride=9), :]
        sb1[j] = stage[...].astype(BF16)
        zt = 4 * c + j

        @pl.when(zt != z)
        def _():
            rdma(sb1.at[j], rb1.at[z], B1 + j, B1 + z, dev(x, y, zt, c)).start()

    add_pair(1)
    for d in (2, 1, 3, 0):
        xt = (x + d) % 4
        for t in range(27):
            pair = []
            for i in (2 * t, 2 * t + 1):
                l, r = divmod(i, 9)
                pair.append(f[l, pl.ds(9 * xt + r, 8, stride=36), :])
            sa1[xt, pl.ds(16 * t, 16), :] = jnp.concatenate(pair, 0).astype(BF16)
        if d:
            rdma(sa1.at[xt], ra1.at[x], A1 + xt, A1 + x, dev(xt, y, z, c)).start()

    @pl.when(act)
    def _():
        for d in range(1, 8):
            zs = (z + d) % 8
            wait_recv(rb1.at[zs], B1 + zs)
        total = sb1[z_lo].astype(F32)
        for d in range(1, 8):
            total += rb1[(z + d) % 8].astype(F32)
        acc_b[pl.ds(0, 224), :] = total
        for d in (2, 1, 3, 0):
            xt = (x + d) % 4
            rows = [acc_b[pl.ds(h * 4 + xt + 64 * i, 8, stride=8), :] for h in range(2) for i in range(4)]
            sb2[xt] = jnp.concatenate(rows, 0).astype(BF16)
            if d:
                rdma(sb2.at[xt], rb2.at[x], B2 + xt, B2 + x, dev(xt, y, z, c)).start()

    for d in range(1, 4):
        xs = (x + d) % 4
        wait_recv(ra1.at[xs], A1 + xs)
    total = sa1[x].astype(F32)
    for d in range(1, 4):
        total += ra1[(x + d) % 4].astype(F32)
    acc_a[pl.ds(0, 432), :] = total
    for j in range(4):
        zt = 4 * c + j
        rows = [acc_a[pl.ds(h * 4 + j + 64 * i, 8, stride=8), :] for h in range(2) for i in range(7)]
        sa2[j] = jnp.concatenate(rows, 0).astype(BF16)

        @pl.when(zt != z)
        def _():
            rdma(sa2.at[j], ra2.at[z], A2 + j, A2 + z, dev(x, y, zt, c)).start()

    @pl.when(act)
    def _():
        for d in range(1, 4):
            xs = (x + d) % 4
            wait_recv(rb2.at[xs], B2 + xs)
        tb = sb2[x].astype(F32)
        for d in range(1, 4):
            tb += rb2[(x + d) % 4].astype(F32)
        for d in range(1, 8):
            zs = (z + d) % 8
            wait_recv(ra2.at[zs], A2 + zs)
        ta = sa2[z_lo].astype(F32)
        for d in range(1, 8):
            ta += ra2[(z + d) % 8].astype(F32)
        for h in range(2):
            s3[h] = jnp.concatenate([ta[h * 56 : h * 56 + 56], tb[h * 32 : h * 32 + 32], jnp.zeros((8, 128), F32)], 0).astype(BF16)
        for d in (4, 3, 5, 2, 6, 1, 7):
            yt = (y + d) % 8
            rdma(s3.at[yt // 4], r3.at[y], Y3 + yt, Y3 + y, dev(x, yt, z, c)).start()
        for d in range(1, 8):
            ys = (y + d) % 8
            wait_recv(r3.at[ys], Y3 + ys)
        g = s3[y_hi].astype(F32)
        for d in range(1, 8):
            g += r3[(y + d) % 8].astype(F32)
        gs[...] = g
        rdma(gs, gs, SIB, SIB, sibling).start()

    @pl.when(jnp.logical_not(act))
    def _():
        wait_recv(gs, SIB)

    steps = jnp.full((9, 128), step[0], jnp.int32).astype(F32)
    first_fix = 1.0 - jnp.exp(steps * math.log(BETA_ONE))
    second_fix = 1.0 - jnp.exp(steps * math.log(BETA_TWO))
    for l in range(9):
        q = l * 9 + (2 if l >= 6 else 0)
        cols = pl.ds(l * 128, 128)
        g = gs[pl.ds(q, 9), :] * (1.0 / 512.0)
        n1 = BETA_ONE * mom1[:, cols] + (1.0 - BETA_ONE) * g
        n2 = BETA_TWO * mom2[:, cols] + (1.0 - BETA_TWO) * g * g
        direction = n1 / first_fix / (jnp.sqrt(n2 / second_fix) + EPSILON)
        nm = master[:, cols] - LEARN_RATE * direction
        o_m1[:, cols] = n1
        o_m2[:, cols] = n2
        o_dir[:, cols] = direction
        o_master[:, cols] = nm
        qs[pl.ds(q, 9), :] = nm

    @pl.when(act)
    def _():
        qs[pl.ds(54, 2), :] = jnp.zeros((2, 128), F32)
        qs[pl.ds(83, 13), :] = jnp.zeros((13, 128), F32)
        pb2[y_hi] = qs[...].astype(BF16)
        rdma(pb2.at[y_hi], pb2.at[y_hi], G1, G1, dev(x, 7 - y, z, c)).start()
        wait_recv(pb2.at[1 - y_hi], G1)
        both = [pb2[h].astype(F32) for h in range(2)]
        gz[z_lo] = jnp.concatenate([b[0:56] for b in both], 0).astype(BF16)
        gx[x] = jnp.concatenate([b[56:88] for b in both], 0).astype(BF16)
        for d in (2, 1, 3):
            xt = (x + d) % 4
            rdma(gx.at[x], gx.at[x], GB2 + xt, GB2 + x, dev(xt, y, z, c)).start()
        for d in (4, 3, 5, 2, 6, 1, 7):
            zt = (z + d) % 8
            rdma(gz.at[z_lo], gz.at[z_lo], GA2 + zt, GA2 + z_lo, dev(x, y, zt, c)).start()
        for d in range(1, 4):
            xs = (x + d) % 4
            wait_recv(gx.at[xs], GB2 + xs)
        for xs in range(4):
            v = gx[xs].astype(F32)
            for h in range(2):
                for i in range(4):
                    acc_b[pl.ds(h * 4 + xs + 64 * i, 8, stride=8), :] = v[h * 32 + i * 8 : h * 32 + i * 8 + 8]
        hb[c, z_lo] = acc_b[pl.ds(0, 224), :].astype(BF16)
        for d in (4, 3, 5, 2, 6, 1, 7):
            zt = (z + d) % 8
            rdma(hb.at[c, z_lo], hb.at[c, z_lo], GB3 + zt, GB3 + z_lo, dev(x, y, zt, c)).start()

    for j in range(4):
        @pl.when(4 * c + j != z)
        def _():
            wait_recv(gz.at[j], GA2 + j)

    for j in range(4):
        v = gz[j].astype(F32)
        for h in range(2):
            for i in range(7):
                acc_a[pl.ds(h * 4 + j + 64 * i, 8, stride=8), :] = v[h * 56 + i * 8 : h * 56 + i * 8 + 8]
    ha[c, x] = acc_a[pl.ds(0, 432), :].astype(BF16)
    for d in (2, 1, 3):
        xt = (x + d) % 4
        rdma(ha.at[c, x], ha.at[c, x], GA3 + xt, GA3 + x, dev(xt, y, z, c)).start()

    def unpack_a(zh, xs):
        v = ha[zh, xs].astype(F32)
        for i in range(54):
            l, r = divmod(i, 9)
            o[zh, l, pl.ds(9 * xs + r, 8, stride=36), :] = v[8 * i : 8 * i + 8]

    def unpack_b(zh, j):
        v = hb[zh, j].astype(F32)
        for i in range(27):
            l, r = divmod(i, 9)
            for h in range(2):
                o[zh, 6 + l, pl.ds(h * 144 + j * 36 + r, 4, stride=9), :] = v[8 * i + 4 * h : 8 * i + 4 * h + 4]

    def pass_on(ref, slot):
        rdma(ref, ref, slot, slot, sibling).start()

    pass_on(ha.at[c, x], FA + x)
    for d in (1, 3, 2):
        xs = (x + d) % 4
        wait_recv(ha.at[c, xs], GA3 + xs)
        pass_on(ha.at[c, xs], FA + xs)
    for j in range(4):
        @pl.when(4 * c + j != z)
        def _():
            wait_recv(hb.at[c, j], GB3 + j)

        pass_on(hb.at[c, j], FB + j)
    for j in range(4):
        unpack_a(c, j)
        unpack_b(c, j)
    for j in range(4):
        wait_recv(ha.at[1 - c, j], FA + j)
        unpack_a(1 - c, j)
    for j in range(4):
        wait_recv(hb.at[1 - c, j], FB + j)
        unpack_b(1 - c, j)
    for zh in range(2):
        for h in range(2):
            for l in range(9):
                o_par[pl.ds(h * 288 + zh * 144, 144), pl.ds(l * 128, 128)] = o[zh, l, pl.ds(h * 144, 144), :].astype(BF16)

    for part in range(2):
        for cp in sib_copies(part):
            cp.wait_send()
    for d in range(1, 4):
        xt = (x + d) % 4
        wait_send(sa1.at[xt], A1 + xt)
        wait_send(ha.at[c, x], GA3 + xt)
    for j in range(4):
        @pl.when(4 * c + j != z)
        def _():
            wait_send(sb1.at[j], B1 + j)
            wait_send(sa2.at[j], A2 + j)

        wait_send(ha.at[c, j], FA + j)
        wait_send(hb.at[c, j], FB + j)

    @pl.when(act)
    def _():
        for d in range(1, 4):
            xt = (x + d) % 4
            wait_send(sb2.at[xt], B2 + xt)
            wait_send(gx.at[x], GB2 + xt)
        for d in range(1, 8):
            yt, zt = (y + d) % 8, (z + d) % 8
            wait_send(s3.at[yt // 4], Y3 + yt)
            wait_send(gz.at[z_lo], GA2 + zt)
            wait_send(hb.at[c, z_lo], GB3 + zt)
        wait_send(gs, SIB)
        wait_send(pb2.at[y_hi], G1)


def local(grad_parts, master, moment_one, moment_two, step_count):
    vm = pl.BlockSpec(memory_space=pltpu.VMEM)
    state = jax.ShapeDtypeStruct((9, D), F32)

    def vb(*shape):
        return pltpu.VMEM(shape, BF16)

    def vf(*shape):
        return pltpu.VMEM(shape, F32)

    return pl.pallas_call(
        kernel,
        out_shape=(state, state, state, state, jax.ShapeDtypeStruct((ROWS, D), BF16)),
        in_specs=[pl.BlockSpec(memory_space=pl.ANY), vm, vm, vm, pl.BlockSpec(memory_space=pltpu.SMEM)],
        out_specs=(vm, vm, vm, vm, vm),
        scratch_shapes=[
            vb(2, 144, D), vb(2, 144, D), vf(9, 288, 128),
            vb(4, 432, 128), vb(4, 432, 128), vb(4, 224, 128), vb(8, 224, 128),
            vf(448, 128), vf(256, 128), vf(224, 128),
            vb(4, 112, 128), vb(8, 112, 128), vb(4, 64, 128), vb(4, 64, 128),
            vb(2, 96, 128), vb(8, 96, 128),
            vf(96, 128), vf(96, 128), vb(2, 96, 128), vb(4, 112, 128), vb(4, 64, 128),
            vb(2, 4, 432, 128), vb(2, 4, 224, 128), vf(2, 9, 288, 128),
            pltpu.SemaphoreType.DMA((END,)), pltpu.SemaphoreType.DMA((END,)),
        ],
        compiler_params=pltpu.CompilerParams(collective_id=0, has_side_effects=True, vmem_limit_bytes=32 * 1024 * 1024),
        name="adam_step",
    )(grad_parts.reshape(ROWS, D), master, moment_one, moment_two, step_count)


def solution(mesh):
    owned = P("shard", None)
    return jax.shard_map(
        local,
        mesh=mesh,
        in_specs=(P("rep", "shard", None, None), owned, owned, owned, P()),
        out_specs=(owned, owned, owned, owned, P()),
        check_vma=False,
    )
```

```python
import math

import jax
import jax.numpy as jnp
from jax import lax
from jax.experimental import pallas as pl
from jax.experimental.pallas import tpu as pltpu
from jax.sharding import PartitionSpec as P

MESH = pl.DeviceIdType.MESH
F32, BF16 = jnp.float32, jnp.bfloat16
BETA_ONE = 0.9
BETA_TWO = 0.95
LEARN_RATE = 0.001
EPSILON = 1e-08

ROWS, D = 576, 1152
VMEM_BYTES = 48_000 * 1024
W = 384
CHUNKS = (2, 0, 1)


def fixes(step):
    steps = jnp.full((9, 128), step[0], jnp.int32).astype(F32)
    return 1.0 - jnp.exp(steps * math.log(BETA_ONE)), 1.0 - jnp.exp(steps * math.log(BETA_TWO))


def adam(total, master, mom1, mom2, first_fix, second_fix):
    g = total * (1.0 / 512.0)
    n1 = BETA_ONE * mom1 + (1.0 - BETA_ONE) * g
    n2 = BETA_TWO * mom2 + (1.0 - BETA_TWO) * g * g
    direction = n1 / first_fix / (jnp.sqrt(n2 / second_fix) + EPSILON)
    return master - LEARN_RATE * direction, n1, n2, direction


def finish(master, mom1, mom2, step, total, params, o_master, o_m1, o_m2, o_dir, o_par, new, sem):
    big = pltpu.make_async_copy(params, o_par, sem.at[3])
    big.start()
    first_fix, second_fix = fixes(step)
    for l in range(9):
        cols = pl.ds(l * 128, 128)
        made = adam(total[:, cols], master[:, cols], mom1[:, cols], mom2[:, cols], first_fix, second_fix)
        for i, v in enumerate(made):
            new[i, :, cols] = v
    outs = [pltpu.make_async_copy(new.at[i], ref, sem.at[4 + i]) for i, ref in enumerate((o_master, o_m1, o_m2, o_dir))]
    for cp in outs:
        cp.start()
    for cp in outs + [big]:
        cp.wait()


def kernel(
    grad, master, mom1, mom2, step,
    gn, out,
    state, own, sib, f, s1, ra1, rb1, acc, stage, s2, ra2, rb2, s3, r3, qs, gz, gx, ha, hb, o,
    send, recv, misc,
):
    rep, shard = lax.axis_index("rep"), lax.axis_index("shard")
    c, y_lo = rep % 2, rep // 2
    x, z, y_hi = shard % 4, (shard // 4) % 8, shard // 32
    y = y_hi * 4 + y_lo
    z_lo = z % 4
    act = z // 4 == c
    idle = jnp.logical_not(act)

    def dev(x_, y_, z_, c_):
        return ((y_ % 4) * 2 + c_, (y_ // 4) * 32 + z_ * 4 + x_)

    sibling = dev(x, y, z, 1 - c)

    barrier = pltpu.get_barrier_semaphore()

    def greet(where):
        pl.semaphore_signal(barrier, inc=1, device_id=where, device_id_type=MESH)

    for d in (4, 3, 5, 2, 6, 1, 7):
        greet(dev(x, y, (z + d) % 8, c))
        greet(dev(x, (y + d) % 8, z, c))
    for d in range(1, 4):
        greet(dev((x + d) % 4, y, z, c))
    greet(sibling)

    ends = {}

    def slot(name, i, n):
        if name not in ends:
            ends[name] = (sum(e[1] for e in ends.values()), n)
        return ends[name][0] + i

    started = []

    def rdma(src, dst, ssem, rsem, where):
        return pltpu.make_async_remote_copy(
            src_ref=src, dst_ref=dst, send_sem=send.at[ssem], recv_sem=recv.at[rsem], device_id=where, device_id_type=MESH
        )

    def push(src, dst, ssem, rsem, where, like, cond=None):
        rdma(src, dst, ssem, rsem, where).start()
        started.append((like, ssem, cond))

    def arrive(ref, rsem):
        rdma(ref, ref, rsem, rsem, sibling).wait_recv()

    def drain():
        for cond in (None, "act", 0, 1, 2, 3):
            mine = [e for e in started if e[2] == cond]
            if not mine:
                continue

            def waits(mine=mine):
                for like, ssem, _ in mine:
                    rdma(like(), like(), ssem, ssem, sibling).wait_send()

            if cond is None:
                waits()
            elif cond == "act":
                pl.when(act)(waits)
            else:
                pl.when(4 * c + cond != z)(waits)

    own_copies = {
        (ch, h): pltpu.make_async_copy(
            grad.at[pl.ds(pl.multiple_of(h * 288 + c * 144, 16), 144), pl.ds(ch * W, W)],
            own.at[h, :, pl.ds(ch * W, W)],
            misc.at[2 * ch + h],
        )
        for ch in CHUNKS
        for h in range(2)
    }
    state_copies = [pltpu.make_async_copy(ref, state.at[y_hi, i], misc.at[6 + i]) for i, ref in enumerate((master, mom1, mom2))]
    for cp in list(own_copies.values()) + state_copies:
        cp.start()
    pl.semaphore_wait(barrier, 18)

    for ch in CHUNKS:
        for h in range(2):
            to = sib.at[h, :, pl.ds(ch * W, W)]
            i = slot("s0", 2 * ch + h, 6)
            push(
                grad.at[pl.ds(pl.multiple_of(h * 288 + (1 - c) * 144, 16), 144), pl.ds(ch * W, W)],
                to, i, i, sibling, lambda to=to: to,
            )

    @pl.when(act)
    def _():
        for i, ref in enumerate((master, mom1, mom2)):
            k = slot("st", i, 3)
            push(ref, state.at[y_hi, i], k, k, dev(x, 7 - y, z, c), lambda: state.at[0, 0], "act")

    for ch in CHUNKS:
        acc[ch, pl.ds(216, 40), :] = jnp.zeros((40, 128), F32)
    stage[pl.ds(216, 8), :] = jnp.zeros((8, 128), F32)
    qs[...] = jnp.zeros((64, 128), F32)

    def add_pair(ch):
        for h in range(2):
            own_copies[ch, h].wait()
            arrive(sib.at[h, :, pl.ds(ch * W, W)], slot("s0", 2 * ch + h, 6))
            for l in range(3 * ch, 3 * ch + 3):
                cols = pl.ds(l * 128, 128)
                f[l, pl.ds(h * 144, 144), :] = own[h, :, cols].astype(F32) + sib[h, :, cols].astype(F32)

    add_pair(2)
    for j in range(4):
        for i in range(27):
            l, r = divmod(i, 9)
            for h in range(2):
                stage[pl.ds(i * 8 + h * 4, 4), :] = f[6 + l, pl.ds(h * 144 + j * 36 + r, 4, stride=9), :]
        s1[2, j] = stage[...].astype(BF16)
        zt = 4 * c + j

        @pl.when(zt != z)
        def _():
            push(s1.at[2, j], rb1.at[z], slot("b1", j, 8), slot("b1", z, 8), dev(x, y, zt, c), lambda: s1.at[2, 0], j)

    for ch in (0, 1):
        add_pair(ch)
        for d in (2, 1, 3, 0):
            xt = (x + d) % 4
            for i in range(27):
                l, r = divmod(i, 9)
                stage[pl.ds(8 * i, 8), :] = f[3 * ch + l, pl.ds(9 * xt + r, 8, stride=36), :]
            s1[ch, d] = stage[...].astype(BF16)
            if d:
                i = slot("a1", 4 * ch + d, 8)
                push(s1.at[ch, d], ra1.at[ch, d], i, i, dev(xt, y, z, c), lambda: s1.at[0, 0])
    def split(ch, t):
        return jnp.concatenate([acc[ch, pl.ds(h * 4 + t + 64 * i, 8, stride=8), :] for h in range(2) for i in range(4)], 0).astype(BF16)

    for ch in (0, 1):
        for d in range(1, 4):
            arrive(ra1.at[ch, d], slot("a1", 4 * ch + d, 8))
        total = s1[ch, 0].astype(F32)
        for d in range(1, 4):
            total += ra1[ch, d].astype(F32)
        acc[ch, pl.ds(0, 224), :] = total
        for j in range(4):
            zt = 4 * c + j
            s2[ch, j] = split(ch, j)

            @pl.when(zt != z)
            def _():
                push(s2.at[ch, j], ra2.at[ch, z], slot("a2", 4 * ch + j, 16), slot("a2", 8 * ch + z, 16), dev(x, y, zt, c), lambda: s2.at[0, 0], j)

    def to_y(ch, total):
        s3[ch] = total.astype(BF16)
        for d in (4, 3, 5, 2, 6, 1, 7):
            k = slot("y", 8 * ch + d, 24)
            push(s3.at[ch], r3.at[ch, d], k, k, dev(x, (y + d) % 8, z, c), lambda: s3.at[0], "act")

    def update(ch):
        for d in range(1, 8):
            arrive(r3.at[ch, d], slot("y", 8 * ch + d, 24))
        total = s3[ch].astype(F32)
        for d in range(1, 8):
            total += r3[ch, d].astype(F32)
        acc[ch, pl.ds(0, 64), :] = total
        for l in range(3):
            cols = pl.ds(ch * W + l * 128, 128)
            gn[:, cols] = acc[ch, pl.ds(pl.multiple_of(y_hi * 32, 32) + l * 9, 9), :]
            for h in range(2):
                qs[pl.ds(h * 32 + l * 9, 9), :] = adam(
                    acc[ch, pl.ds(h * 32 + l * 9, 9), :], state[h, 0, :, cols], state[h, 1, :, cols], state[h, 2, :, cols], *fixed
                )[0]
        return qs[...].astype(BF16)

    def z_gather(ch):
        gz[ch, z_lo] = update(ch)
        for d in (4, 3, 5, 2, 6, 1, 7):
            push(
                gz.at[ch, z_lo], gz.at[ch, z_lo], slot("ga2", 8 * ch + d, 16), slot("ga2", 8 * ch + z_lo, 16),
                dev(x, y, (z + d) % 8, c), lambda: gz.at[0, 0], "act",
            )

    def join(ch, blocks):
        for t in range(4):
            v = blocks[t].astype(F32)
            for h in range(2):
                for i in range(4):
                    acc[ch, pl.ds(h * 4 + t + 64 * i, 8, stride=8), :] = v[h * 32 + i * 8 : h * 32 + i * 8 + 8]
        return acc[ch, pl.ds(0, 224), :].astype(BF16)

    fixed = fixes(step)
    for cp in state_copies:
        cp.wait()

    @pl.when(act)
    def _():
        for d in range(1, 8):
            arrive(rb1.at[(z + d) % 8], slot("b1", (z + d) % 8, 8))
        total = s1[2, z_lo].astype(F32)
        for d in range(1, 8):
            total += rb1[(z + d) % 8].astype(F32)
        acc[2, pl.ds(0, 224), :] = total
        for d in (2, 1, 3, 0):
            xt = (x + d) % 4
            s2[2, d] = split(2, xt)
            if d:
                k = slot("b2", d, 4)
                push(s2.at[2, d], rb2.at[d], k, k, dev(xt, y, z, c), lambda: s2.at[0, 0], "act")

        for ch in (0, 2, 1):
            if ch == 2:
                for d in range(1, 4):
                    arrive(rb2.at[d], slot("b2", d, 4))
                total = s2[2, 0].astype(F32)
                for d in range(1, 4):
                    total += rb2[d].astype(F32)
            else:
                for d in range(1, 8):
                    arrive(ra2.at[ch, (z + d) % 8], slot("a2", 8 * ch + (z + d) % 8, 16))
                total = s2[ch, z_lo].astype(F32)
                for d in range(1, 8):
                    total += ra2[ch, (z + d) % 8].astype(F32)
            to_y(ch, total)

        for i in range(3):
            arrive(state.at[1 - y_hi, i], slot("st", i, 3))
        z_gather(0)
        gx[x] = update(2)
        for d in (2, 1, 3):
            push(gx.at[x], gx.at[x], slot("gb2", d, 4), slot("gb2", x, 4), dev((x + d) % 4, y, z, c), lambda: gx.at[0], "act")
        z_gather(1)
        k = slot("g", 0, 1)
        push(gn, gn, k, k, sibling, lambda: gn, "act")

        for d in range(1, 4):
            arrive(gx.at[(x + d) % 4], slot("gb2", (x + d) % 4, 4))
        hb[c, z_lo] = join(2, [gx[t] for t in range(4)])
        for d in (4, 3, 5, 2, 6, 1, 7):
            push(
                hb.at[c, z_lo], hb.at[c, z_lo], slot("gb3", d, 8), slot("gb3", z_lo, 8),
                dev(x, y, (z + d) % 8, c), lambda: hb.at[0, 0], "act",
            )

    for ch in (0, 1):
        for j in range(4):
            @pl.when(4 * c + j != z)
            def _():
                arrive(gz.at[ch, j], slot("ga2", 8 * ch + j, 16))

        ha[ch, c, x] = join(ch, [gz[ch, t] for t in range(4)])
        mine = ha.at[ch, c, x]
        for d in (2, 1, 3):
            push(mine, mine, slot("ga3", 4 * ch + d, 8), slot("ga3", 4 * ch + x, 8), dev((x + d) % 4, y, z, c), lambda: ha.at[0, 0, 0])
        push(mine, mine, slot("fa", 4 * ch, 8), slot("fa", 4 * ch + x, 8), sibling, lambda: ha.at[0, 0, 0])

    def unpack_a(ch, zh, xs):
        v = ha[ch, zh, xs].astype(F32)
        for i in range(27):
            l, r = divmod(i, 9)
            o[zh, 3 * ch + l, pl.ds(9 * xs + r, 8, stride=36), :] = v[8 * i : 8 * i + 8]

    def unpack_b(zh, j):
        v = hb[zh, j].astype(F32)
        for i in range(27):
            l, r = divmod(i, 9)
            for h in range(2):
                o[zh, 6 + l, pl.ds(h * 144 + j * 36 + r, 4, stride=9), :] = v[8 * i + 4 * h : 8 * i + 4 * h + 4]

    for ch in (0, 1):
        for d in (1, 3, 2):
            xs = (x + d) % 4
            ref = ha.at[ch, c, xs]
            arrive(ref, slot("ga3", 4 * ch + xs, 8))
            push(ref, ref, slot("fa", 4 * ch + d, 8), slot("fa", 4 * ch + xs, 8), sibling, lambda: ha.at[0, 0, 0])
        for t in range(4):
            unpack_a(ch, c, t)
    for j in range(4):
        @pl.when(4 * c + j != z)
        def _():
            arrive(hb.at[c, j], slot("gb3", j, 8))

        k = slot("fb", j, 4)
        push(hb.at[c, j], hb.at[c, j], k, k, sibling, lambda: hb.at[0, 0])
    for j in range(4):
        unpack_b(c, j)

    def write(ch):
        for l in range(3 * ch, 3 * ch + 3):
            for zh in range(2):
                for h in range(2):
                    out[pl.ds(h * 288 + zh * 144, 144), pl.ds(l * 128, 128)] = o[zh, l, pl.ds(h * 144, 144), :].astype(BF16)

    @pl.when(idle)
    def _():
        arrive(gn, slot("g", 0, 1))

    for ch in (0, 1):
        for t in range(4):
            arrive(ha.at[ch, 1 - c, t], slot("fa", 4 * ch + t, 8))
            unpack_a(ch, 1 - c, t)
        write(ch)
    for j in range(4):
        arrive(hb.at[1 - c, j], slot("fb", j, 4))
        unpack_b(1 - c, j)
    write(2)
    drain()


N_SEM = 160


def local(grad_parts, master, moment_one, moment_two, step_count):
    hbm = pl.BlockSpec(memory_space=pltpu.HBM)
    sm = pl.BlockSpec(memory_space=pltpu.SMEM)
    vm = pl.BlockSpec(memory_space=pltpu.VMEM)
    state = jax.ShapeDtypeStruct((9, D), F32)
    weights = jax.ShapeDtypeStruct((ROWS, D), BF16)

    def vb(*shape):
        return pltpu.VMEM(shape, BF16)

    def vf(*shape):
        return pltpu.VMEM(shape, F32)

    gradient = pltpu.with_memory_space_constraint(grad_parts.reshape(ROWS, D), pltpu.HBM)
    held = [pltpu.with_memory_space_constraint(a, pltpu.HBM) for a in (master, moment_one, moment_two)]
    summed, params = pl.pallas_call(
        kernel,
        out_shape=(state, weights),
        in_specs=[hbm, hbm, hbm, hbm, sm],
        out_specs=(vm, vm),
        scratch_shapes=[
            vf(2, 3, 9, D), vb(2, 144, D), vb(2, 144, D), vf(9, 288, 128),
            vb(3, 4, 224, 128), vb(2, 4, 224, 128), vb(8, 224, 128), vf(3, 256, 128), vf(224, 128),
            vb(3, 4, 64, 128), vb(2, 8, 64, 128), vb(4, 64, 128), vb(3, 64, 128), vb(3, 8, 64, 128),
            vf(64, 128), vb(2, 4, 64, 128), vb(4, 64, 128),
            vb(2, 2, 4, 224, 128), vb(2, 4, 224, 128), vf(2, 9, 288, 128),
            pltpu.SemaphoreType.DMA((N_SEM,)), pltpu.SemaphoreType.DMA((N_SEM,)), pltpu.SemaphoreType.DMA((13,)),
        ],
        compiler_params=pltpu.CompilerParams(collective_id=0, has_side_effects=True, vmem_limit_bytes=VMEM_BYTES),
        name="reduce_update_gather",
    )(gradient, *held, step_count)
    return pl.pallas_call(
        finish,
        out_shape=(state, state, state, state, weights),
        in_specs=[vm, vm, vm, sm, vm, vm],
        out_specs=(hbm,) * 5,
        scratch_shapes=[vf(4, 9, D), pltpu.SemaphoreType.DMA((8,))],
        compiler_params=pltpu.CompilerParams(vmem_limit_bytes=VMEM_BYTES),
        name="write_out",
    )(master, moment_one, moment_two, step_count, summed, params)


def solution(mesh):
    owned = P("shard", None)
    return jax.shard_map(
        local,
        mesh=mesh,
        in_specs=(P("rep", "shard", None, None), owned, owned, owned, P()),
        out_specs=(owned, owned, owned, owned, P()),
        check_vma=False,
    )
```

```python
import math

import jax
import jax.numpy as jnp
from jax import lax
from jax.experimental import pallas as pl
from jax.experimental.pallas import tpu as pltpu
from jax.sharding import PartitionSpec as P

MESH = pl.DeviceIdType.MESH
F32, BF16 = jnp.float32, jnp.bfloat16
BETA_ONE = 0.9
BETA_TWO = 0.95
LEARN_RATE = 0.001
EPSILON = 1e-08

ROWS, D = 576, 1152
VMEM_BYTES = 48_000 * 1024
W = 384
CHUNKS = (2, 0, 1)


def fixes(step):
    steps = jnp.full((9, 128), step[0], jnp.int32).astype(F32)
    return 1.0 - jnp.exp(steps * math.log(BETA_ONE)), 1.0 - jnp.exp(steps * math.log(BETA_TWO))


def adam(total, master, mom1, mom2, first_fix, second_fix):
    g = total * (1.0 / 512.0)
    n1 = BETA_ONE * mom1 + (1.0 - BETA_ONE) * g
    n2 = BETA_TWO * mom2 + (1.0 - BETA_TWO) * g * g
    direction = n1 / first_fix / (jnp.sqrt(n2 / second_fix) + EPSILON)
    return master - LEARN_RATE * direction, n1, n2, direction


def finish(master, mom1, mom2, step, total, params, o_master, o_m1, o_m2, o_dir, o_par, new, sem):
    big = pltpu.make_async_copy(params, o_par, sem.at[3])
    big.start()
    first_fix, second_fix = fixes(step)
    for l in range(9):
        cols = pl.ds(l * 128, 128)
        made = adam(total[:, cols], master[:, cols], mom1[:, cols], mom2[:, cols], first_fix, second_fix)
        for i, v in enumerate(made):
            new[i, :, cols] = v
    outs = [pltpu.make_async_copy(new.at[i], ref, sem.at[4 + i]) for i, ref in enumerate((o_master, o_m1, o_m2, o_dir))]
    for cp in outs:
        cp.start()
    for cp in outs + [big]:
        cp.wait()


def kernel(
    grad, master, mom1, mom2, step,
    gn, out,
    state, own, sib, f, s1, ra1, rb1, acc, stage, s2, ra2, rb2, s3, r3, qs, gz, gx, ha, hb, o,
    send, recv, misc, here, ready,
):
    rep, shard = lax.axis_index("rep"), lax.axis_index("shard")
    c, y_lo = rep % 2, rep // 2
    x, z, y_hi = shard % 4, (shard // 4) % 8, shard // 32
    y = y_hi * 4 + y_lo
    z_lo = z % 4
    act = z // 4 == c
    idle = jnp.logical_not(act)

    def dev(x_, y_, z_, c_):
        return ((y_ % 4) * 2 + c_, (y_ // 4) * 32 + z_ * 4 + x_)

    sibling = dev(x, y, z, 1 - c)

    names = {}

    def sem(name, i=0):
        return names.setdefault((name, i), len(names))

    def rdma(src, dst, ssem, rsem, where):
        return pltpu.make_async_remote_copy(
            src_ref=src, dst_ref=dst, send_sem=send.at[ssem], recv_sem=recv.at[rsem], device_id=where, device_id_type=MESH
        )

    def push(src, dst, out_sem, in_sem, where):
        rdma(src, dst, out_sem, in_sem, where).start()

    def arrive(like, in_sem):
        rdma(like, like, 0, in_sem, sibling).wait_recv()

    def sent(like, out_sem):
        rdma(like, like, out_sem, 0, sibling).wait_send()

    barrier = pltpu.get_barrier_semaphore()

    def tell(sem_ref, where):
        pl.semaphore_signal(sem_ref, inc=1, device_id=where, device_id_type=MESH)

    def push_pair(ch):
        push(grad.at[:, 1 - c, :, pl.ds(ch * W, W)], sib.at[:, :, pl.ds(ch * W, W)], sem("s0"), sem("s0", ch), sibling)

    @pl.when(c == 1)
    def _():
        tell(barrier, sibling)

    @pl.when(c == 0)
    def _():
        pl.semaphore_wait(barrier, 1)
        tell(here, sibling)
        for d in (4, 3, 5, 2, 6, 1, 7):
            tell(barrier, dev(x, y, (z + d) % 8, 1))

    @pl.when(c == 1)
    def _():
        pl.semaphore_wait(here, 1)
        for d in (2, 1, 3):
            tell(barrier, dev((x + d) % 4, y, z, 1))
        for d in (4, 3, 5, 2, 6, 1, 7):
            tell(barrier, dev(x, (y + d) % 8, z, 1))

    def all_here():
        @pl.when(c == 1)
        def _():
            pl.semaphore_wait(barrier, 17)
            tell(ready, sibling)

        @pl.when(c == 0)
        def _():
            pl.semaphore_wait(ready, 1)

    for ch in CHUNKS:
        push_pair(ch)

    own_copies = [
        pltpu.make_async_copy(grad.at[:, c, :, pl.ds(ch * W, W)], own.at[:, :, pl.ds(ch * W, W)], misc.at[ch]) for ch in range(3)
    ]
    state_copies = [pltpu.make_async_copy(ref, state.at[y_hi, i], misc.at[3 + i]) for i, ref in enumerate((master, mom1, mom2))]
    for ch in CHUNKS:
        own_copies[ch].start()
    for cp in state_copies:
        cp.start()
    for ch in CHUNKS:
        acc[ch, pl.ds(216, 40), :] = jnp.zeros((40, 128), F32)
    stage[pl.ds(216, 8), :] = jnp.zeros((8, 128), F32)
    qs[...] = jnp.zeros((64, 128), F32)

    def add_pair(ch):
        own_copies[ch].wait()
        arrive(sib.at[:, :, pl.ds(ch * W, W)], sem("s0", ch))
        for h in range(2):
            for l in range(3 * ch, 3 * ch + 3):
                cols = pl.ds(l * 128, 128)
                f[l, pl.ds(h * 144, 144), :] = own[h, :, cols].astype(F32) + sib[h, :, cols].astype(F32)

    add_pair(2)
    for j in range(4):
        for i in range(27):
            l, r = divmod(i, 9)
            for h in range(2):
                stage[pl.ds(i * 8 + h * 4, 4), :] = f[6 + l, pl.ds(h * 144 + j * 36 + r, 4, stride=9), :]
        s1[2, j] = stage[...].astype(BF16)
        if j == 0:
            all_here()
        zt = 4 * c + j

        @pl.when(zt != z)
        def _():
            push(s1.at[2, j], rb1.at[z], sem("b1"), sem("b1"), dev(x, y, zt, c))

    for ch in (0, 1):
        add_pair(ch)
        for d in (2, 1, 3, 0):
            xt = (x + d) % 4
            for i in range(27):
                l, r = divmod(i, 9)
                stage[pl.ds(8 * i, 8), :] = f[3 * ch + l, pl.ds(9 * xt + r, 8, stride=36), :]
            s1[ch, d] = stage[...].astype(BF16)
            if d:
                push(s1.at[ch, d], ra1.at[ch, d - 1], sem("a1"), sem("a1", ch), dev(xt, y, z, c))
    @pl.when(act)
    def _():
        for i, ref in enumerate((master, mom1, mom2)):
            push(ref, state.at[y_hi, i], sem("st", i), sem("st", i), dev(x, 7 - y, z, c))

    def split(ch, t):
        return jnp.concatenate([acc[ch, pl.ds(h * 4 + t + 64 * i, 8, stride=8), :] for h in range(2) for i in range(4)], 0).astype(BF16)

    for ch in (0, 1):
        arrive(ra1.at[ch], sem("a1", ch))
        total = s1[ch, 0].astype(F32)
        for d in range(3):
            total += ra1[ch, d].astype(F32)
        acc[ch, pl.ds(0, 224), :] = total
        for j in range(4):
            zt = 4 * c + j
            s2[ch, j] = split(ch, j)

            @pl.when(zt != z)
            def _():
                push(s2.at[ch, j], ra2.at[ch, z], sem("a2"), sem("a2", ch), dev(x, y, zt, c))

    def to_y(ch, total):
        s3[ch] = total.astype(BF16)
        for d in (4, 3, 5, 2, 6, 1, 7):
            push(s3.at[ch], r3.at[ch, d - 1], sem("y"), sem("y", ch), dev(x, (y + d) % 8, z, c))

    def update(ch):
        arrive(r3.at[ch], sem("y", ch))
        total = s3[ch].astype(F32)
        for d in range(7):
            total += r3[ch, d].astype(F32)
        acc[ch, pl.ds(0, 64), :] = total
        for l in range(3):
            cols = pl.ds(ch * W + l * 128, 128)
            gn[:, cols] = acc[ch, pl.ds(pl.multiple_of(y_hi * 32, 32) + l * 9, 9), :]
            for h in range(2):
                qs[pl.ds(h * 32 + l * 9, 9), :] = adam(
                    acc[ch, pl.ds(h * 32 + l * 9, 9), :], state[h, 0, :, cols], state[h, 1, :, cols], state[h, 2, :, cols], *fixed
                )[0]
        return qs[...].astype(BF16)

    def z_gather(ch):
        gz[ch, z_lo] = update(ch)
        for d in (4, 3, 5, 2, 6, 1, 7):
            push(gz.at[ch, z_lo], gz.at[ch, z_lo], sem("ga2"), sem("ga2", ch), dev(x, y, (z + d) % 8, c))

    def join(ch, blocks):
        for t in range(4):
            v = blocks[t].astype(F32)
            for h in range(2):
                for i in range(4):
                    acc[ch, pl.ds(h * 4 + t + 64 * i, 8, stride=8), :] = v[h * 32 + i * 8 : h * 32 + i * 8 + 8]
        return acc[ch, pl.ds(0, 224), :].astype(BF16)

    fixed = fixes(step)
    for cp in state_copies:
        cp.wait()

    @pl.when(act)
    def _():
        arrive(rb1.at[pl.ds(0, 7)], sem("b1"))
        total = s1[2, z_lo].astype(F32)
        for d in range(1, 8):
            total += rb1[(z + d) % 8].astype(F32)
        acc[2, pl.ds(0, 224), :] = total
        for d in (2, 1, 3, 0):
            xt = (x + d) % 4
            s2[2, d] = split(2, xt)
            if d:
                push(s2.at[2, d], rb2.at[d - 1], sem("b2"), sem("b2"), dev(xt, y, z, c))

        for ch in (0, 2, 1):
            if ch == 2:
                arrive(rb2, sem("b2"))
                total = s2[2, 0].astype(F32)
                for d in range(3):
                    total += rb2[d].astype(F32)
            else:
                arrive(ra2.at[ch, pl.ds(0, 7)], sem("a2", ch))
                total = s2[ch, z_lo].astype(F32)
                for d in range(1, 8):
                    total += ra2[ch, (z + d) % 8].astype(F32)
            to_y(ch, total)

        for i in range(3):
            arrive(state.at[1 - y_hi, i], sem("st", i))
        z_gather(0)
        gx[x] = update(2)
        for d in (2, 1, 3):
            push(gx.at[x], gx.at[x], sem("gb2"), sem("gb2"), dev((x + d) % 4, y, z, c))
        z_gather(1)
        push(gn, gn, sem("g"), sem("g"), sibling)

        arrive(gx.at[pl.ds(0, 3)], sem("gb2"))
        hb[c, z_lo] = join(2, [gx[t] for t in range(4)])
        for d in (4, 3, 5, 2, 6, 1, 7):
            push(hb.at[c, z_lo], hb.at[c, z_lo], sem("gb3"), SEM_Z + z_lo, dev(x, y, (z + d) % 8, c))

    for ch in (0, 1):
        @pl.when(act)
        def _():
            arrive(gz.at[ch, pl.ds(0, 3)], sem("ga2", ch))

        @pl.when(idle)
        def _():
            arrive(gz.at[ch], sem("ga2", ch))

        ha[ch, c, x] = join(ch, [gz[ch, t] for t in range(4)])
        mine = ha.at[ch, c, x]
        for d in (2, 1, 3):
            push(mine, mine, sem("ga3"), SEM_X + 4 * ch + x, dev((x + d) % 4, y, z, c))
        push(mine, mine, sem("fa"), sem("fa", ch), sibling)

    def unpack_a(ch, zh, xs):
        v = ha[ch, zh, xs].astype(F32)
        for i in range(27):
            l, r = divmod(i, 9)
            o[zh, 3 * ch + l, pl.ds(9 * xs + r, 8, stride=36), :] = v[8 * i : 8 * i + 8]

    def unpack_b(zh, j):
        v = hb[zh, j].astype(F32)
        for i in range(27):
            l, r = divmod(i, 9)
            for h in range(2):
                o[zh, 6 + l, pl.ds(h * 144 + j * 36 + r, 4, stride=9), :] = v[8 * i + 4 * h : 8 * i + 4 * h + 4]

    for ch in (0, 1):
        for d in (1, 3, 2):
            xs = (x + d) % 4
            ref = ha.at[ch, c, xs]
            arrive(ref, SEM_X + 4 * ch + xs)
            push(ref, ref, sem("fa"), sem("fa", ch), sibling)
        for t in range(4):
            unpack_a(ch, c, t)
    for j in range(4):
        @pl.when(4 * c + j != z)
        def _():
            arrive(hb.at[c, j], SEM_Z + j)

        push(hb.at[c, j], hb.at[c, j], sem("fb"), sem("fb"), sibling)
    for j in range(4):
        unpack_b(c, j)

    def write(ch):
        for l in range(3 * ch, 3 * ch + 3):
            for zh in range(2):
                for h in range(2):
                    out[pl.ds(h * 288 + zh * 144, 144), pl.ds(l * 128, 128)] = o[zh, l, pl.ds(h * 144, 144), :].astype(BF16)

    @pl.when(idle)
    def _():
        arrive(gn, sem("g"))

    for ch in (0, 1):
        arrive(ha.at[ch, 1 - c], sem("fa", ch))
        for t in range(4):
            unpack_a(ch, 1 - c, t)
        write(ch)
    arrive(hb.at[1 - c], sem("fb"))
    for j in range(4):
        unpack_b(1 - c, j)
    write(2)

    sent(sib, sem("s0"))
    sent(ha.at[:, 0, pl.ds(0, 3)], sem("a1"))
    sent(ha.at[:, 0, pl.ds(0, 3)], sem("ga3"))
    sent(ha.at[:, 0], sem("fa"))
    sent(hb.at[0], sem("fb"))

    @pl.when(idle)
    def _():
        sent(s1.at[2], sem("b1"))
        sent(s2.at[pl.ds(0, 2)], sem("a2"))

    @pl.when(act)
    def _():
        sent(s1.at[2, pl.ds(0, 3)], sem("b1"))
        sent(s2.at[pl.ds(0, 2), pl.ds(0, 3)], sem("a2"))
        for i in range(3):
            sent(state.at[0, i], sem("st", i))
        sent(rb2, sem("b2"))
        sent(r3, sem("y"))
        sent(ra2.at[:, pl.ds(0, 7)], sem("ga2"))
        sent(rb2, sem("gb2"))
        sent(rb1.at[pl.ds(0, 7)], sem("gb3"))
        sent(gn, sem("g"))


N_SEM = 36
SEM_X, SEM_Z = 24, 32


def local(grad_parts, master, moment_one, moment_two, step_count):
    hbm = pl.BlockSpec(memory_space=pltpu.HBM)
    sm = pl.BlockSpec(memory_space=pltpu.SMEM)
    vm = pl.BlockSpec(memory_space=pltpu.VMEM)
    state = jax.ShapeDtypeStruct((9, D), F32)
    weights = jax.ShapeDtypeStruct((ROWS, D), BF16)

    def vb(*shape):
        return pltpu.VMEM(shape, BF16)

    def vf(*shape):
        return pltpu.VMEM(shape, F32)

    gradient = pltpu.with_memory_space_constraint(grad_parts.reshape(2, 2, 144, D), pltpu.HBM)
    held = [pltpu.with_memory_space_constraint(a, pltpu.HBM) for a in (master, moment_one, moment_two)]
    summed, params = pl.pallas_call(
        kernel,
        out_shape=(state, weights),
        in_specs=[hbm, hbm, hbm, hbm, sm],
        out_specs=(vm, vm),
        scratch_shapes=[
            vf(2, 3, 9, D), vb(2, 144, D), vb(2, 144, D), vf(9, 288, 128),
            vb(3, 4, 224, 128), vb(2, 3, 224, 128), vb(8, 224, 128), vf(3, 256, 128), vf(224, 128),
            vb(3, 4, 64, 128), vb(2, 8, 64, 128), vb(3, 64, 128), vb(3, 64, 128), vb(3, 7, 64, 128),
            vf(64, 128), vb(2, 4, 64, 128), vb(4, 64, 128),
            vb(2, 2, 4, 224, 128), vb(2, 4, 224, 128), vf(2, 9, 288, 128),
            pltpu.SemaphoreType.DMA((N_SEM,)), pltpu.SemaphoreType.DMA((N_SEM,)), pltpu.SemaphoreType.DMA((6,)),
            pltpu.SemaphoreType.REGULAR, pltpu.SemaphoreType.REGULAR,
        ],
        compiler_params=pltpu.CompilerParams(collective_id=0, has_side_effects=True, vmem_limit_bytes=VMEM_BYTES),
        name="reduce_update_gather",
    )(gradient, *held, step_count)
    return pl.pallas_call(
        finish,
        out_shape=(state, state, state, state, weights),
        in_specs=[vm, vm, vm, sm, vm, vm],
        out_specs=(hbm,) * 5,
        scratch_shapes=[vf(4, 9, D), pltpu.SemaphoreType.DMA((8,))],
        compiler_params=pltpu.CompilerParams(vmem_limit_bytes=VMEM_BYTES),
        name="write_out",
    )(master, moment_one, moment_two, step_count, summed, params)


def solution(mesh):
    owned = P("shard", None)
    return jax.shard_map(
        local,
        mesh=mesh,
        in_specs=(P("rep", "shard", None, None), owned, owned, owned, P()),
        out_specs=(owned, owned, owned, owned, P()),
        check_vma=False,
    )
```

```python
import math

import jax
import jax.numpy as jnp
from jax import lax
from jax.experimental import pallas as pl
from jax.experimental.pallas import tpu as pltpu
from jax.sharding import PartitionSpec as P

MESH = pl.DeviceIdType.MESH
F32, BF16 = jnp.float32, jnp.bfloat16
BETA_ONE = 0.9
BETA_TWO = 0.95
LEARN_RATE = 0.001
EPSILON = 1e-08

ROWS, D = 576, 1152
VMEM_BYTES = 48_000 * 1024
CHUNKS = ((0, 3, "A"), (3, 2, "A"), (5, 2, "A"), (7, 2, "B"))
FIRST = (3, 0, 1, 2)
MIDDLE = (0, 3, 1, 2)
LAST = (0, 1, 2, 3)
IN_A = tuple(i for i, ch in enumerate(CHUNKS) if ch[2] == "A")
IN_B = tuple(i for i, ch in enumerate(CHUNKS) if ch[2] == "B")
GROUPS = tuple(n for _, n, _ in CHUNKS)
LONG = tuple(-(-72 * n // 16) * 16 for n in GROUPS)
HALF = tuple(-(-9 * n // 8) * 8 for n in GROUPS)
SHORT = tuple(2 * n for n in HALF)

SEM_LAST = 4 + 7 * len(CHUNKS)


def columns(ch):
    return pl.ds(CHUNKS[ch][0] * 128, CHUNKS[ch][1] * 128)


def scratch():
    found = {
        "state": ((2, 3, 9, D), F32), "own": ((2, 144, D), BF16), "sib": ((2, 144, D), BF16), "f": ((9, 288, 128), F32),
        "gn": None, "o": ((2, 9, 288, 128), F32),
    }
    for ch, (_, n, kind) in enumerate(CHUNKS):
        long, short = (LONG[ch], 128), (SHORT[ch], 128)
        found |= {
            f"acc{ch}": ((8 * HALF[ch] + 64, 128), F32), f"qs{ch}": (short, F32), f"stage{ch}": (long, F32),
            f"s1_{ch}": ((4,) + long, BF16), f"s2_{ch}": ((4,) + short, BF16), f"s3_{ch}": (short, BF16), f"r3_{ch}": ((7,) + short, BF16),
            f"r1_{ch}": ((3 if kind == "A" else 8,) + long, BF16), f"r2_{ch}": ((8 if kind == "A" else 3,) + short, BF16),
            f"g1_{ch}": ((4,) + short, BF16), f"g2_{ch}": ((2, 4) + long, BF16),
        }
    return {name: kind for name, kind in found.items() if kind}


def fixes(step):
    steps = jnp.full((9, 128), step[0], jnp.int32).astype(F32)
    return 1.0 - jnp.exp(steps * math.log(BETA_ONE)), 1.0 - jnp.exp(steps * math.log(BETA_TWO))


def adam(total, master, mom1, mom2, first_fix, second_fix):
    g = total * (1.0 / 512.0)
    n1 = BETA_ONE * mom1 + (1.0 - BETA_ONE) * g
    n2 = BETA_TWO * mom2 + (1.0 - BETA_TWO) * g * g
    direction = n1 / first_fix / (jnp.sqrt(n2 / second_fix) + EPSILON)
    return master - LEARN_RATE * direction, n1, n2, direction


def finish(master, mom1, mom2, step, total, params, o_master, o_m1, o_m2, o_dir, o_par, new, sem):
    big = pltpu.make_async_copy(params, o_par, sem.at[3])
    big.start()
    first_fix, second_fix = fixes(step)
    for l in range(9):
        cols = pl.ds(l * 128, 128)
        made = adam(total[:, cols], master[:, cols], mom1[:, cols], mom2[:, cols], first_fix, second_fix)
        for i, v in enumerate(made):
            new[i, :, cols] = v
    outs = [pltpu.make_async_copy(new.at[i], ref, sem.at[4 + i]) for i, ref in enumerate((o_master, o_m1, o_m2, o_dir))]
    for cp in outs:
        cp.start()
    for cp in outs + [big]:
        cp.wait()


def kernel(grad, master, mom1, mom2, step, gn, out, *refs):
    names = tuple(scratch())
    b = dict(zip(names, refs))
    send, recv, misc, here, ready = refs[len(names):]
    state, own, sib, f, o = (b[name] for name in ("state", "own", "sib", "f", "o"))

    def of(name):
        return [b[f"{name}{ch}"] for ch in range(len(CHUNKS))]

    acc, qs, stage = of("acc"), of("qs"), of("stage")
    s1, s2, s3, r1, r2, r3, g1, g2 = (of(name) for name in ("s1_", "s2_", "s3_", "r1_", "r2_", "r3_", "g1_", "g2_"))
    rep, shard = lax.axis_index("rep"), lax.axis_index("shard")
    c, y_lo = rep % 2, rep // 2
    x, z, y_hi = shard % 4, (shard // 4) % 8, shard // 32
    y = y_hi * 4 + y_lo
    z_lo = z % 4
    act = z // 4 == c
    idle = jnp.logical_not(act)

    def dev(x_, y_, z_, c_):
        return ((y_ % 4) * 2 + c_, (y_ // 4) * 32 + z_ * 4 + x_)

    sibling = dev(x, y, z, 1 - c)

    numbers = {}

    def sem(name, i=0):
        return numbers.setdefault((name, i), len(numbers))

    def rdma(src, dst, ssem, rsem, where):
        return pltpu.make_async_remote_copy(
            src_ref=src, dst_ref=dst, send_sem=send.at[ssem], recv_sem=recv.at[rsem], device_id=where, device_id_type=MESH
        )

    def push(src, dst, out_sem, in_sem, where):
        rdma(src, dst, out_sem, in_sem, where).start()

    def arrive(like, in_sem):
        rdma(like, like, 0, in_sem, sibling).wait_recv()

    def sent(like, out_sem):
        rdma(like, like, out_sem, 0, sibling).wait_send()

    barrier = pltpu.get_barrier_semaphore()

    def tell(sem_ref, where):
        pl.semaphore_signal(sem_ref, inc=1, device_id=where, device_id_type=MESH)

    def push_pair(ch):
        push(grad.at[:, 1 - c, :, columns(ch)], sib.at[:, :, columns(ch)], sem("s0"), sem("s0", ch), sibling)

    @pl.when(c == 1)
    def _():
        tell(barrier, sibling)

    @pl.when(c == 0)
    def _():
        pl.semaphore_wait(barrier, 1)
        tell(here, sibling)
        push_pair(FIRST[0])
        for d in (4, 3, 5, 2, 6, 1, 7):
            tell(barrier, dev(x, y, (z + d) % 8, 1))

    @pl.when(c == 1)
    def _():
        pl.semaphore_wait(here, 1)
        push_pair(FIRST[0])
        for d in (2, 1, 3):
            tell(barrier, dev((x + d) % 4, y, z, 1))
        for d in (4, 3, 5, 2, 6, 1, 7):
            tell(barrier, dev(x, (y + d) % 8, z, 1))

    def all_here():
        @pl.when(c == 1)
        def _():
            pl.semaphore_wait(barrier, 17)
            tell(ready, sibling)

        @pl.when(c == 0)
        def _():
            pl.semaphore_wait(ready, 1)

    for ch in FIRST[1:]:
        push_pair(ch)

    n_ch = len(CHUNKS)
    own_copies = [
        pltpu.make_async_copy(grad.at[:, c, :, columns(ch)], own.at[:, :, columns(ch)], misc.at[ch]) for ch in range(n_ch)
    ]
    state_copies = [pltpu.make_async_copy(ref, state.at[y_hi, i], misc.at[n_ch + i]) for i, ref in enumerate((master, mom1, mom2))]
    for ch in FIRST:
        own_copies[ch].start()
    for cp in state_copies:
        cp.start()
    for ch in range(n_ch):
        used = 72 * GROUPS[ch]
        acc[ch][pl.ds(used, acc[ch].shape[0] - used), :] = jnp.zeros((acc[ch].shape[0] - used, 128), F32)
        if LONG[ch] > used:
            stage[ch][pl.ds(used, LONG[ch] - used), :] = jnp.zeros((LONG[ch] - used, 128), F32)
        qs[ch][...] = jnp.zeros((SHORT[ch], 128), F32)

    def add_pair(ch):
        own_copies[ch].wait()
        arrive(sib.at[:, :, columns(ch)], sem("s0", ch))
        first, n, _ = CHUNKS[ch]
        for h in range(2):
            for l in range(first, first + n):
                cols = pl.ds(l * 128, 128)
                f[l, pl.ds(h * 144, 144), :] = own[h, :, cols].astype(F32) + sib[h, :, cols].astype(F32)

    for turn, ch in enumerate(FIRST):
        add_pair(ch)
        if turn == 0:
            all_here()
        first, n, kind = CHUNKS[ch]
        if kind == "B":
            for j in range(4):
                for i in range(9 * n):
                    l, r = divmod(i, 9)
                    for h in range(2):
                        stage[ch][pl.ds(i * 8 + h * 4, 4), :] = f[first + l, pl.ds(h * 144 + j * 36 + r, 4, stride=9), :]
                s1[ch][j] = stage[ch][...].astype(BF16)
                zt = 4 * c + j

                @pl.when(zt != z)
                def _():
                    push(s1[ch].at[j], r1[ch].at[z], sem("b1", ch), sem("b1", ch), dev(x, y, zt, c))
        else:
            for d in (2, 1, 3, 0):
                xt = (x + d) % 4
                for i in range(9 * n):
                    l, r = divmod(i, 9)
                    stage[ch][pl.ds(8 * i, 8), :] = f[first + l, pl.ds(9 * xt + r, 8, stride=36), :]
                s1[ch][d] = stage[ch][...].astype(BF16)
                if d:
                    push(s1[ch].at[d], r1[ch].at[d - 1], sem("a1", ch), sem("a1", ch), dev(xt, y, z, c))

    @pl.when(act)
    def _():
        for i, ref in enumerate((master, mom1, mom2)):
            push(ref, state.at[y_hi, i], sem("st", i), sem("st", i), dev(x, 7 - y, z, c))

    def split(ch, t):
        rows = [acc[ch][pl.ds(h * 4 + t + 64 * i, 8, stride=8), :] for h in range(2) for i in range(HALF[ch] // 8)]
        return jnp.concatenate(rows, 0).astype(BF16)

    def add_up(ch, mine, theirs, which):
        total = mine.astype(F32)
        for i in which:
            total += theirs[i].astype(F32)
        return total

    for ch in IN_A:
        arrive(r1[ch], sem("a1", ch))
        acc[ch][pl.ds(0, LONG[ch]), :] = add_up(ch, s1[ch][0], r1[ch], range(3))
        for j in range(4):
            zt = 4 * c + j
            s2[ch][j] = split(ch, j)

            @pl.when(zt != z)
            def _():
                push(s2[ch].at[j], r2[ch].at[z], sem("a2", ch), sem("a2", ch), dev(x, y, zt, c))

    def others_z():
        return [(z + d) % 8 for d in range(1, 8)]

    def to_y(ch, total):
        s3[ch][...] = total.astype(BF16)
        for d in (4, 3, 5, 2, 6, 1, 7):
            push(s3[ch], r3[ch].at[d - 1], sem("y", ch), sem("y", ch), dev(x, (y + d) % 8, z, c))

    def update(ch):
        arrive(r3[ch], sem("y", ch))
        acc[ch][pl.ds(0, SHORT[ch]), :] = add_up(ch, s3[ch][...], r3[ch], range(7))
        first, n, _ = CHUNKS[ch]
        half = HALF[ch]
        for l in range(n):
            cols = pl.ds((first + l) * 128, 128)
            gn[:, cols] = acc[ch][pl.ds(pl.multiple_of(y_hi * half, 8) + l * 9, 9), :]
            for h in range(2):
                qs[ch][pl.ds(h * half + l * 9, 9), :] = adam(
                    acc[ch][pl.ds(h * half + l * 9, 9), :], state[h, 0, :, cols], state[h, 1, :, cols], state[h, 2, :, cols], *fixed
                )[0]
        return qs[ch][...].astype(BF16)

    def join(ch):
        half = HALF[ch]
        for t in range(4):
            v = g1[ch][t].astype(F32)
            for h in range(2):
                for i in range(half // 8):
                    acc[ch][pl.ds(h * 4 + t + 64 * i, 8, stride=8), :] = v[h * half + i * 8 : h * half + i * 8 + 8]
        return acc[ch][pl.ds(0, LONG[ch]), :].astype(BF16)

    fixed = fixes(step)
    for cp in state_copies:
        cp.wait()

    @pl.when(act)
    def _():
        for ch in IN_B:
            arrive(r1[ch].at[pl.ds(0, 7)], sem("b1", ch))
            acc[ch][pl.ds(0, LONG[ch]), :] = add_up(ch, s1[ch][z_lo], r1[ch], others_z())
            for d in (2, 1, 3, 0):
                xt = (x + d) % 4
                s2[ch][d] = split(ch, xt)
                if d:
                    push(s2[ch].at[d], r2[ch].at[d - 1], sem("b2", ch), sem("b2", ch), dev(xt, y, z, c))

        for ch in MIDDLE:
            if ch in IN_B:
                arrive(r2[ch], sem("b2", ch))
                to_y(ch, add_up(ch, s2[ch][0], r2[ch], range(3)))
            else:
                arrive(r2[ch].at[pl.ds(0, 7)], sem("a2", ch))
                to_y(ch, add_up(ch, s2[ch][z_lo], r2[ch], others_z()))

        for i in range(3):
            arrive(state.at[1 - y_hi, i], sem("st", i))
        for ch in MIDDLE:
            if ch in IN_B:
                g1[ch][x] = update(ch)
                for d in (2, 1, 3):
                    push(g1[ch].at[x], g1[ch].at[x], sem("gb2", ch), sem("gb2", ch), dev((x + d) % 4, y, z, c))
            else:
                g1[ch][z_lo] = update(ch)
                for d in (4, 3, 5, 2, 6, 1, 7):
                    push(g1[ch].at[z_lo], g1[ch].at[z_lo], sem("ga2", ch), sem("ga2", ch), dev(x, y, (z + d) % 8, c))
        push(gn, gn, sem("g"), sem("g"), sibling)

        for k, ch in enumerate(IN_B):
            arrive(g1[ch].at[pl.ds(0, 3)], sem("gb2", ch))
            g2[ch][c, z_lo] = join(ch)
            for d in (4, 3, 5, 2, 6, 1, 7):
                push(g2[ch].at[c, z_lo], g2[ch].at[c, z_lo], sem("gb3", ch), SEM_LAST + 4 * ch + z_lo, dev(x, y, (z + d) % 8, c))

    for ch in IN_A:
        @pl.when(act)
        def _():
            arrive(g1[ch].at[pl.ds(0, 3)], sem("ga2", ch))

        @pl.when(idle)
        def _():
            arrive(g1[ch], sem("ga2", ch))

        g2[ch][c, x] = join(ch)
        mine = g2[ch].at[c, x]
        for d in (2, 1, 3):
            push(mine, mine, sem("ga3", ch), SEM_LAST + 4 * ch + x, dev((x + d) % 4, y, z, c))
        push(mine, mine, sem("f", ch), sem("f", ch), sibling)

    def unpack(ch, zh, t):
        first, n, kind = CHUNKS[ch]
        v = g2[ch][zh, t].astype(F32)
        for i in range(9 * n):
            l, r = divmod(i, 9)
            if kind == "A":
                o[zh, first + l, pl.ds(9 * t + r, 8, stride=36), :] = v[8 * i : 8 * i + 8]
            else:
                for h in range(2):
                    o[zh, first + l, pl.ds(h * 144 + t * 36 + r, 4, stride=9), :] = v[8 * i + 4 * h : 8 * i + 4 * h + 4]

    for ch in LAST:
        if ch in IN_A:
            for d in (1, 3, 2):
                xs = (x + d) % 4
                ref = g2[ch].at[c, xs]
                arrive(ref, SEM_LAST + 4 * ch + xs)
                push(ref, ref, sem("f", ch), sem("f", ch), sibling)
        else:
            for j in range(4):
                ref = g2[ch].at[c, j]

                @pl.when(4 * c + j != z)
                def _():
                    arrive(ref, SEM_LAST + 4 * ch + j)

                push(ref, ref, sem("f", ch), sem("f", ch), sibling)
        for t in range(4):
            unpack(ch, c, t)

    @pl.when(idle)
    def _():
        arrive(gn, sem("g"))

    for ch in LAST:
        arrive(g2[ch].at[1 - c], sem("f", ch))
        for t in range(4):
            unpack(ch, 1 - c, t)
        first, n, _ = CHUNKS[ch]
        for l in range(first, first + n):
            for zh in range(2):
                for h in range(2):
                    out[pl.ds(h * 288 + zh * 144, 144), pl.ds(l * 128, 128)] = o[zh, l, pl.ds(h * 144, 144), :].astype(BF16)

    sent(sib, sem("s0"))
    for ch in range(n_ch):
        sent(g2[ch].at[0], sem("f", ch))
    for ch in IN_A:
        sent(r1[ch], sem("a1", ch))
        sent(r1[ch], sem("ga3", ch))

    @pl.when(idle)
    def _():
        for ch in IN_A:
            sent(s2[ch], sem("a2", ch))
        for ch in IN_B:
            sent(s1[ch], sem("b1", ch))

    @pl.when(act)
    def _():
        for i in range(3):
            sent(state.at[0, i], sem("st", i))
        for ch in IN_A:
            sent(s2[ch].at[pl.ds(0, 3)], sem("a2", ch))
            sent(r3[ch], sem("ga2", ch))
        for ch in IN_B:
            sent(s1[ch].at[pl.ds(0, 3)], sem("b1", ch))
            sent(r2[ch], sem("b2", ch))
            sent(r2[ch], sem("gb2", ch))
            sent(r1[ch].at[pl.ds(0, 7)], sem("gb3", ch))
        for ch in range(n_ch):
            sent(r3[ch], sem("y", ch))
        sent(gn, sem("g"))

    if len(numbers) > SEM_LAST:
        raise ValueError(len(numbers))


N_SEM = SEM_LAST + 4 * len(CHUNKS)


def local(grad_parts, master, moment_one, moment_two, step_count):
    hbm = pl.BlockSpec(memory_space=pltpu.HBM)
    sm = pl.BlockSpec(memory_space=pltpu.SMEM)
    vm = pl.BlockSpec(memory_space=pltpu.VMEM)
    state = jax.ShapeDtypeStruct((9, D), F32)
    weights = jax.ShapeDtypeStruct((ROWS, D), BF16)

    def vf(*shape):
        return pltpu.VMEM(shape, F32)

    gradient = pltpu.with_memory_space_constraint(grad_parts.reshape(2, 2, 144, D), pltpu.HBM)
    held = [pltpu.with_memory_space_constraint(a, pltpu.HBM) for a in (master, moment_one, moment_two)]
    summed, params = pl.pallas_call(
        kernel,
        out_shape=(state, weights),
        in_specs=[hbm, hbm, hbm, hbm, sm],
        out_specs=(vm, vm),
        scratch_shapes=[
            *(pltpu.VMEM(*kind) for kind in scratch().values()),
            pltpu.SemaphoreType.DMA((SEM_LAST,)), pltpu.SemaphoreType.DMA((N_SEM,)), pltpu.SemaphoreType.DMA((3 + len(CHUNKS),)),
            pltpu.SemaphoreType.REGULAR, pltpu.SemaphoreType.REGULAR,
        ],
        compiler_params=pltpu.CompilerParams(collective_id=0, has_side_effects=True, vmem_limit_bytes=VMEM_BYTES),
        name="reduce_update_gather",
    )(gradient, *held, step_count)
    return pl.pallas_call(
        finish,
        out_shape=(state, state, state, state, weights),
        in_specs=[vm, vm, vm, sm, vm, vm],
        out_specs=(hbm,) * 5,
        scratch_shapes=[vf(4, 9, D), pltpu.SemaphoreType.DMA((8,))],
        compiler_params=pltpu.CompilerParams(vmem_limit_bytes=VMEM_BYTES),
        name="write_out",
    )(master, moment_one, moment_two, step_count, summed, params)


def solution(mesh):
    owned = P("shard", None)
    return jax.shard_map(
        local,
        mesh=mesh,
        in_specs=(P("rep", "shard", None, None), owned, owned, owned, P()),
        out_specs=(owned, owned, owned, owned, P()),
        check_vma=False,
    )
```

```python
import math

import jax
import jax.numpy as jnp
from jax import lax
from jax.experimental import pallas as pl
from jax.experimental.pallas import tpu as pltpu
from jax.sharding import PartitionSpec as P

MESH = pl.DeviceIdType.MESH
F32, BF16 = jnp.float32, jnp.bfloat16
BETA_ONE = 0.9
BETA_TWO = 0.95
LEARN_RATE = 0.001
EPSILON = 1e-08

ROWS, D = 576, 1152
VMEM_BYTES = 48_000 * 1024
CHUNKS = ((0, 3, "A"), (3, 2, "A"), (5, 2, "A"), (7, 2, "B"))
FIRST = (3, 0, 1, 2)
MIDDLE = (0, 3, 1, 2)
LAST = (0, 1, 3, 2)
IN_A = tuple(i for i, ch in enumerate(CHUNKS) if ch[2] == "A")
IN_B = tuple(i for i, ch in enumerate(CHUNKS) if ch[2] == "B")
GROUPS = tuple(n for _, n, _ in CHUNKS)
LONG = tuple(-(-72 * n // 16) * 16 for n in GROUPS)
HALF = tuple(-(-9 * n // 8) * 8 for n in GROUPS)
SHORT = tuple(2 * n for n in HALF)

SEM_LAST = 4 + 7 * len(CHUNKS)


def columns(ch):
    return pl.ds(CHUNKS[ch][0] * 128, CHUNKS[ch][1] * 128)


def scratch():
    found = {
        "state": ((2, 3, 9, D), F32), "own": ((2, 144, D), BF16), "sib": ((2, 144, D), BF16), "f": ((9, 288, 128), F32),
        "gn": None, "o": ((2, 9, 288, 128), F32),
    }
    for ch, (_, n, kind) in enumerate(CHUNKS):
        long, short = (LONG[ch], 128), (SHORT[ch], 128)
        found |= {
            f"acc{ch}": ((8 * HALF[ch] + 64, 128), F32), f"qs{ch}": (short, F32), f"stage{ch}": (long, F32),
            f"s1_{ch}": ((4,) + long, BF16), f"s2_{ch}": ((4,) + short, BF16), f"s3_{ch}": (short, BF16), f"r3_{ch}": ((7,) + short, BF16),
            f"r1_{ch}": ((3 if kind == "A" else 8,) + long, BF16), f"r2_{ch}": ((8 if kind == "A" else 3,) + short, BF16),
            f"g1_{ch}": ((4,) + short, BF16), f"g2_{ch}": ((2, 4) + long, BF16),
        }
    return {name: kind for name, kind in found.items() if kind}


def fixes(step):
    steps = jnp.full((9, 128), step[0], jnp.int32).astype(F32)
    return 1.0 - jnp.exp(steps * math.log(BETA_ONE)), 1.0 - jnp.exp(steps * math.log(BETA_TWO))


def adam(total, master, mom1, mom2, first_fix, second_fix):
    g = total * (1.0 / 512.0)
    n1 = BETA_ONE * mom1 + (1.0 - BETA_ONE) * g
    n2 = BETA_TWO * mom2 + (1.0 - BETA_TWO) * g * g
    direction = n1 / first_fix / (jnp.sqrt(n2 / second_fix) + EPSILON)
    return master - LEARN_RATE * direction, n1, n2, direction


def finish(master, mom1, mom2, step, total, params, o_master, o_m1, o_m2, o_dir, o_par, new, sem):
    big = pltpu.make_async_copy(params, o_par, sem.at[3])
    big.start()
    first_fix, second_fix = fixes(step)
    for l in range(9):
        cols = pl.ds(l * 128, 128)
        made = adam(total[:, cols], master[:, cols], mom1[:, cols], mom2[:, cols], first_fix, second_fix)
        for i, v in enumerate(made):
            new[i, :, cols] = v
    outs = [pltpu.make_async_copy(new.at[i], ref, sem.at[4 + i]) for i, ref in enumerate((o_master, o_m1, o_m2, o_dir))]
    for cp in outs:
        cp.start()
    for cp in outs + [big]:
        cp.wait()


def kernel(grad, master, mom1, mom2, step, gn, out, *refs):
    names = tuple(scratch())
    b = dict(zip(names, refs))
    send, recv, misc, here, ready = refs[len(names):]
    state, own, sib, f, o = (b[name] for name in ("state", "own", "sib", "f", "o"))

    def of(name):
        return [b[f"{name}{ch}"] for ch in range(len(CHUNKS))]

    acc, qs, stage = of("acc"), of("qs"), of("stage")
    s1, s2, s3, r1, r2, r3, g1, g2 = (of(name) for name in ("s1_", "s2_", "s3_", "r1_", "r2_", "r3_", "g1_", "g2_"))
    rep, shard = lax.axis_index("rep"), lax.axis_index("shard")
    rem, div = lax.rem, lax.div
    c, y_lo = rem(rep, 2), div(rep, 2)
    x, z, y_hi = rem(shard, 4), rem(div(shard, 4), 8), div(shard, 32)
    y = y_hi * 4 + y_lo
    z_lo = rem(z, 4)
    act = div(z, 4) == c
    idle = jnp.logical_not(act)

    sibling = (y_lo * 2 + 1 - c, shard)
    xs_at = [rem(x + d, 4) for d in range(4)]
    zs_at = [rem(z + d, 8) for d in range(8)]
    ys_at = [rem(y + d, 8) for d in range(8)]
    chips_x = [(y_lo, y_hi * 32 + z * 4 + i) for i in xs_at]
    chips_z = [(y_lo, y_hi * 32 + i * 4 + x) for i in zs_at]
    chips_y = [(rem(i, 4), div(i, 4) * 32 + z * 4 + x) for i in ys_at]
    at_x, at_z, at_y = ([(i * 2 + c, j) for i, j in chips] for chips in (chips_x, chips_z, chips_y))
    greet_x, greet_z, greet_y = ([(i * 2 + 1, j) for i, j in chips] for chips in (chips_x, chips_z, chips_y))
    owners = [(rep, y_hi * 32 + (4 * c + j) * 4 + x) for j in range(4)]
    mirror = ((3 - y_lo) * 2 + c, (1 - y_hi) * 32 + z * 4 + x)

    numbers = {}

    def sem(name, i=0):
        return numbers.setdefault((name, i), len(numbers))

    def rdma(src, dst, ssem, rsem, where):
        return pltpu.make_async_remote_copy(
            src_ref=src, dst_ref=dst, send_sem=send.at[ssem], recv_sem=recv.at[rsem], device_id=where, device_id_type=MESH
        )

    def push(src, dst, out_sem, in_sem, where):
        rdma(src, dst, out_sem, in_sem, where).start()

    def arrive(like, in_sem):
        rdma(like, like, 0, in_sem, sibling).wait_recv()

    def sent(like, out_sem):
        rdma(like, like, out_sem, 0, sibling).wait_send()

    barrier = pltpu.get_barrier_semaphore()

    def tell(sem_ref, where):
        pl.semaphore_signal(sem_ref, inc=1, device_id=where, device_id_type=MESH)

    def push_pair(ch):
        push(grad.at[:, 1 - c, :, columns(ch)], sib.at[:, :, columns(ch)], sem("s0"), sem("s0", ch), sibling)

    @pl.when(c == 1)
    def _():
        tell(barrier, sibling)

    @pl.when(c == 0)
    def _():
        pl.semaphore_wait(barrier, 1)
        tell(here, sibling)
        push_pair(FIRST[0])
        for d in (4, 3, 5, 2, 6, 1, 7):
            tell(barrier, greet_z[d])

    @pl.when(c == 1)
    def _():
        pl.semaphore_wait(here, 1)
        push_pair(FIRST[0])
        for d in (2, 1, 3):
            tell(barrier, greet_x[d])
        for d in (4, 3, 5, 2, 6, 1, 7):
            tell(barrier, greet_y[d])

    def all_here():
        @pl.when(c == 1)
        def _():
            pl.semaphore_wait(barrier, 17)
            tell(ready, sibling)

        @pl.when(c == 0)
        def _():
            pl.semaphore_wait(ready, 1)

    for ch in FIRST[1:]:
        push_pair(ch)

    n_ch = len(CHUNKS)
    own_copies = [
        pltpu.make_async_copy(grad.at[:, c, :, columns(ch)], own.at[:, :, columns(ch)], misc.at[ch]) for ch in range(n_ch)
    ]
    state_copies = [pltpu.make_async_copy(ref, state.at[y_hi, i], misc.at[n_ch + i]) for i, ref in enumerate((master, mom1, mom2))]
    for ch in FIRST:
        own_copies[ch].start()
    for cp in state_copies:
        cp.start()
    for ch in range(n_ch):
        used = 72 * GROUPS[ch]
        acc[ch][pl.ds(used, acc[ch].shape[0] - used), :] = jnp.zeros((acc[ch].shape[0] - used, 128), F32)
        if LONG[ch] > used:
            stage[ch][pl.ds(used, LONG[ch] - used), :] = jnp.zeros((LONG[ch] - used, 128), F32)
        qs[ch][...] = jnp.zeros((SHORT[ch], 128), F32)

    def add_pair(ch):
        own_copies[ch].wait()
        arrive(sib.at[:, :, columns(ch)], sem("s0", ch))
        first, n, _ = CHUNKS[ch]
        for h in range(2):
            for l in range(first, first + n):
                cols = pl.ds(l * 128, 128)
                f[l, pl.ds(h * 144, 144), :] = own[h, :, cols].astype(F32) + sib[h, :, cols].astype(F32)

    for turn, ch in enumerate(FIRST):
        add_pair(ch)
        if turn == 0:
            all_here()
        first, n, kind = CHUNKS[ch]
        if kind == "B":
            for j in range(4):
                for i in range(9 * n):
                    l, r = divmod(i, 9)
                    for h in range(2):
                        stage[ch][pl.ds(i * 8 + h * 4, 4), :] = f[first + l, pl.ds(h * 144 + j * 36 + r, 4, stride=9), :]
                s1[ch][j] = stage[ch][...].astype(BF16)
                zt = 4 * c + j

                @pl.when(zt != z)
                def _():
                    push(s1[ch].at[j], r1[ch].at[z], sem("b1", ch), sem("b1", ch), owners[j])
        else:
            for d in (2, 1, 3, 0):
                xt = xs_at[d]
                for i in range(9 * n):
                    l, r = divmod(i, 9)
                    stage[ch][pl.ds(8 * i, 8), :] = f[first + l, pl.ds(9 * xt + r, 8, stride=36), :]
                s1[ch][d] = stage[ch][...].astype(BF16)
                if d:
                    push(s1[ch].at[d], r1[ch].at[d - 1], sem("a1", ch), sem("a1", ch), at_x[d])

    @pl.when(act)
    def _():
        for i, ref in enumerate((master, mom1, mom2)):
            push(ref, state.at[y_hi, i], sem("st", i), sem("st", i), mirror)

    def split(ch, t):
        rows = [acc[ch][pl.ds(h * 4 + t + 64 * i, 8, stride=8), :] for h in range(2) for i in range(HALF[ch] // 8)]
        return jnp.concatenate(rows, 0).astype(BF16)

    def add_up(ch, mine, theirs, which):
        total = mine.astype(F32)
        for i in which:
            total += theirs[i].astype(F32)
        return total

    for ch in IN_A:
        arrive(r1[ch], sem("a1", ch))
        acc[ch][pl.ds(0, LONG[ch]), :] = add_up(ch, s1[ch][0], r1[ch], range(3))
        for j in range(4):
            zt = 4 * c + j
            s2[ch][j] = split(ch, j)

            @pl.when(zt != z)
            def _():
                push(s2[ch].at[j], r2[ch].at[z], sem("a2", ch), sem("a2", ch), owners[j])

    def others_z():
        return zs_at[1:]

    def to_y(ch, total):
        s3[ch][...] = total.astype(BF16)
        for d in (4, 3, 5, 2, 6, 1, 7):
            push(s3[ch], r3[ch].at[d - 1], sem("y", ch), sem("y", ch), at_y[d])

    def update(ch):
        arrive(r3[ch], sem("y", ch))
        acc[ch][pl.ds(0, SHORT[ch]), :] = add_up(ch, s3[ch][...], r3[ch], range(7))
        first, n, _ = CHUNKS[ch]
        half = HALF[ch]
        for l in range(n):
            cols = pl.ds((first + l) * 128, 128)
            gn[:, cols] = acc[ch][pl.ds(pl.multiple_of(y_hi * half, 8) + l * 9, 9), :]
            for h in range(2):
                qs[ch][pl.ds(h * half + l * 9, 9), :] = adam(
                    acc[ch][pl.ds(h * half + l * 9, 9), :], state[h, 0, :, cols], state[h, 1, :, cols], state[h, 2, :, cols], *fixed
                )[0]
        return qs[ch][...].astype(BF16)

    def join(ch):
        half = HALF[ch]
        for t in range(4):
            v = g1[ch][t].astype(F32)
            for h in range(2):
                for i in range(half // 8):
                    acc[ch][pl.ds(h * 4 + t + 64 * i, 8, stride=8), :] = v[h * half + i * 8 : h * half + i * 8 + 8]
        return acc[ch][pl.ds(0, LONG[ch]), :].astype(BF16)

    fixed = fixes(step)
    for cp in state_copies:
        cp.wait()

    @pl.when(act)
    def _():
        for ch in IN_B:
            arrive(r1[ch].at[pl.ds(0, 7)], sem("b1", ch))
            acc[ch][pl.ds(0, LONG[ch]), :] = add_up(ch, s1[ch][z_lo], r1[ch], others_z())
            for d in (2, 1, 3, 0):
                xt = xs_at[d]
                s2[ch][d] = split(ch, xt)
                if d:
                    push(s2[ch].at[d], r2[ch].at[d - 1], sem("b2", ch), sem("b2", ch), at_x[d])

        for ch in MIDDLE:
            if ch in IN_B:
                arrive(r2[ch], sem("b2", ch))
                to_y(ch, add_up(ch, s2[ch][0], r2[ch], range(3)))
            else:
                arrive(r2[ch].at[pl.ds(0, 7)], sem("a2", ch))
                to_y(ch, add_up(ch, s2[ch][z_lo], r2[ch], others_z()))

        for i in range(3):
            arrive(state.at[1 - y_hi, i], sem("st", i))
        for ch in MIDDLE:
            if ch in IN_B:
                g1[ch][x] = update(ch)
                for d in (2, 1, 3):
                    push(g1[ch].at[x], g1[ch].at[x], sem("gb2", ch), sem("gb2", ch), at_x[d])
            else:
                g1[ch][z_lo] = update(ch)
                for d in (4, 3, 5, 2, 6, 1, 7):
                    push(g1[ch].at[z_lo], g1[ch].at[z_lo], sem("ga2", ch), sem("ga2", ch), at_z[d])
        push(gn, gn, sem("g"), sem("g"), sibling)

        for k, ch in enumerate(IN_B):
            arrive(g1[ch].at[pl.ds(0, 3)], sem("gb2", ch))
            g2[ch][c, z_lo] = join(ch)
            for d in (4, 3, 5, 2, 6, 1, 7):
                push(g2[ch].at[c, z_lo], g2[ch].at[c, z_lo], sem("gb3", ch), SEM_LAST + 4 * ch + z_lo, at_z[d])

    for ch in IN_A:
        @pl.when(act)
        def _():
            arrive(g1[ch].at[pl.ds(0, 3)], sem("ga2", ch))

        @pl.when(idle)
        def _():
            arrive(g1[ch], sem("ga2", ch))

        g2[ch][c, x] = join(ch)
        mine = g2[ch].at[c, x]
        for d in (2, 1, 3):
            push(mine, mine, sem("ga3", ch), SEM_LAST + 4 * ch + x, at_x[d])
        push(mine, mine, sem("f", ch), sem("f", ch), sibling)

    def unpack(ch, zh, t):
        first, n, kind = CHUNKS[ch]
        v = g2[ch][zh, t].astype(F32)
        for i in range(9 * n):
            l, r = divmod(i, 9)
            if kind == "A":
                o[zh, first + l, pl.ds(9 * t + r, 8, stride=36), :] = v[8 * i : 8 * i + 8]
            else:
                for h in range(2):
                    o[zh, first + l, pl.ds(h * 144 + t * 36 + r, 4, stride=9), :] = v[8 * i + 4 * h : 8 * i + 4 * h + 4]

    for ch in LAST:
        if ch in IN_A:
            for d in (1, 3, 2):
                xs = xs_at[d]
                ref = g2[ch].at[c, xs]
                arrive(ref, SEM_LAST + 4 * ch + xs)
                push(ref, ref, sem("f", ch), sem("f", ch), sibling)
        else:
            for j in range(4):
                ref = g2[ch].at[c, j]

                @pl.when(4 * c + j != z)
                def _():
                    arrive(ref, SEM_LAST + 4 * ch + j)

                push(ref, ref, sem("f", ch), sem("f", ch), sibling)
        for t in range(4):
            unpack(ch, c, t)

    @pl.when(idle)
    def _():
        arrive(gn, sem("g"))

    for ch in LAST:
        arrive(g2[ch].at[1 - c], sem("f", ch))
        for t in range(4):
            unpack(ch, 1 - c, t)
        first, n, _ = CHUNKS[ch]
        for l in range(first, first + n):
            for zh in range(2):
                for h in range(2):
                    out[pl.ds(h * 288 + zh * 144, 144), pl.ds(l * 128, 128)] = o[zh, l, pl.ds(h * 144, 144), :].astype(BF16)

    sent(sib, sem("s0"))
    for ch in range(n_ch):
        sent(g2[ch].at[0], sem("f", ch))
    for ch in IN_A:
        sent(r1[ch], sem("a1", ch))
        sent(r1[ch], sem("ga3", ch))

    @pl.when(idle)
    def _():
        for ch in IN_A:
            sent(s2[ch], sem("a2", ch))
        for ch in IN_B:
            sent(s1[ch], sem("b1", ch))

    @pl.when(act)
    def _():
        for i in range(3):
            sent(state.at[0, i], sem("st", i))
        for ch in IN_A:
            sent(s2[ch].at[pl.ds(0, 3)], sem("a2", ch))
            sent(r3[ch], sem("ga2", ch))
        for ch in IN_B:
            sent(s1[ch].at[pl.ds(0, 3)], sem("b1", ch))
            sent(r2[ch], sem("b2", ch))
            sent(r2[ch], sem("gb2", ch))
            sent(r1[ch].at[pl.ds(0, 7)], sem("gb3", ch))
        for ch in range(n_ch):
            sent(r3[ch], sem("y", ch))
        sent(gn, sem("g"))

    if len(numbers) > SEM_LAST:
        raise ValueError(len(numbers))


N_SEM = SEM_LAST + 4 * len(CHUNKS)


def local(grad_parts, master, moment_one, moment_two, step_count):
    hbm = pl.BlockSpec(memory_space=pltpu.HBM)
    sm = pl.BlockSpec(memory_space=pltpu.SMEM)
    vm = pl.BlockSpec(memory_space=pltpu.VMEM)
    state = jax.ShapeDtypeStruct((9, D), F32)
    weights = jax.ShapeDtypeStruct((ROWS, D), BF16)

    def vf(*shape):
        return pltpu.VMEM(shape, F32)

    gradient = pltpu.with_memory_space_constraint(grad_parts.reshape(2, 2, 144, D), pltpu.HBM)
    held = [pltpu.with_memory_space_constraint(a, pltpu.HBM) for a in (master, moment_one, moment_two)]
    summed, params = pl.pallas_call(
        kernel,
        out_shape=(state, weights),
        in_specs=[hbm, hbm, hbm, hbm, sm],
        out_specs=(vm, vm),
        scratch_shapes=[
            *(pltpu.VMEM(*kind) for kind in scratch().values()),
            pltpu.SemaphoreType.DMA((SEM_LAST,)), pltpu.SemaphoreType.DMA((N_SEM,)), pltpu.SemaphoreType.DMA((3 + len(CHUNKS),)),
            pltpu.SemaphoreType.REGULAR, pltpu.SemaphoreType.REGULAR,
        ],
        compiler_params=pltpu.CompilerParams(collective_id=0, has_side_effects=True, vmem_limit_bytes=VMEM_BYTES),
        name="reduce_update_gather",
    )(gradient, *held, step_count)
    return pl.pallas_call(
        finish,
        out_shape=(state, state, state, state, weights),
        in_specs=[vm, vm, vm, sm, vm, vm],
        out_specs=(hbm,) * 5,
        scratch_shapes=[vf(4, 9, D), pltpu.SemaphoreType.DMA((8,))],
        compiler_params=pltpu.CompilerParams(vmem_limit_bytes=VMEM_BYTES),
        name="write_out",
    )(master, moment_one, moment_two, step_count, summed, params)


def solution(mesh):
    owned = P("shard", None)
    return jax.shard_map(
        local,
        mesh=mesh,
        in_specs=(P("rep", "shard", None, None), owned, owned, owned, P()),
        out_specs=(owned, owned, owned, owned, P()),
        check_vma=False,
    )
```
